256 devices in a mesh: dp: 32 (over z_hi, x, core), tensor: 8 (over y, z_lo).
Axes of the slice: x: 4, y: 4, z: 8 (z_hi: 4, z_lo: 2; z = z_hi * 2 + z_lo), core: 2. Of those that a mesh axis runs over, the one named last changes fastest.
Arguments:
- query_acts: bfloat16 [1024, 5120], P(None, 'dp'), may hold values from -6 to 6
- query_pos: int32 [64], replicated, may hold values from 0 to 1023
- query_feat: int32 [64], replicated, may hold values from 0 to 127
- sae_enc: bfloat16 [128, 27648], P(None, 'tensor'), may hold values from -6 to 6
- basis_in: bfloat16 [5120, 5120], P('dp', 'tensor'), may hold values from -0.078125 to 0.078125
- basis_out: bfloat16 [27648, 27648], P('tensor', 'dp'), may hold values from -0.0390625 to 0.0390625
- eigvals: float32 [5120, 27648], P('tensor', 'dp'), may hold values from 0.05 to 900, as said below
- train_in: bfloat16 [32, 32, 5120], P('dp', None, 'tensor'), may hold values from -6 to 6
- train_out: bfloat16 [32, 32, 27648], P('dp'), may hold values from -6 to 6
Outputs:
- influence: float32 [64, 32], P(None, 'dp')
The draws below stay inside these ranges and needn't reach their ends.
Inputs may be any that keep to these rules, and one draw needn't show every extreme that they name: eigvals are positive.
All inputs are finite; a program needn't handle non-finite values.
Results may differ from the reference program's by a relative error of at most 0.0075.
Values may be sent and summed in bfloat16 or wider, within the bound.
A program may use at most 128 MiB of HBM per device.

```python
import math
import jax
import jax.numpy as jnp
from jax import lax

DIN = 5120
DOUT = 27648
R = 32
QUERIES = 64
CTX = 1024
NMON = 128
SEQS = 32


def draw_eigvals(key, part):
    key = jax.random.fold_in(key, 7)
    first, second, third = jax.random.split(key, 3)
    base = jnp.exp(jax.random.uniform(first, (DIN, DOUT), jnp.float32, math.log(0.05), 0.0))
    rows = 3.0 ** (jnp.arange(DIN, dtype=jnp.float32) / (DIN - 1)) * 10.0 ** jax.random.uniform(second, (DIN,), jnp.float32)
    cols = 3.0 ** (jnp.arange(DOUT, dtype=jnp.float32) / (DOUT - 1)) * 10.0 ** jax.random.uniform(third, (DOUT,), jnp.float32)
    return base * rows[:, None] * cols[None, :]


def with_ends(entries, key, low, high):
    longest = entries.shape.index(max(entries.shape))
    spots = []
    for shift in (0, 1):
        where = [jax.random.randint(jax.random.fold_in(key, axis), (), 0, length) for axis, length in enumerate(entries.shape)]
        where[longest] = (where[longest] + shift) % entries.shape[longest]
        spots.append(tuple(where))
    return entries.at[spots[0]].set(low).at[spots[1]].set(high)


def steps_of(stream_key, dims, pieces, smallest, top_value):
    level, own = 1.0, jax.random.fold_in(stream_key, 6)
    for position, shards_of in pieces:
        heights = jnp.exp(jax.random.uniform(jax.random.fold_in(own, position), (shards_of,), jnp.float32, smallest / len(pieces), top_value / len(pieces)))
        level = level * jnp.repeat(heights, dims[position] // shards_of).reshape([-1 if axis == position else 1 for axis in range(len(dims))])
    return level


def noise(stream_key, dims, scale, bound, cuts=(), kind=jnp.bfloat16):
    gain = steps_of(stream_key, dims, cuts, -0.22, 0.18) if cuts else 1.0
    result = jax.random.normal(stream_key, dims, jnp.float32) * scale * gain
    return jnp.minimum(jnp.maximum(result, -bound), bound).astype(kind)


def setup_inputs(seed: int = 0) -> dict:
    streams_of = jax.random.split(jax.random.key(seed), 10)
    query_acts = noise(streams_of[0], (CTX, DIN), 1.0, 6.0, ((1, 32),))
    query_pos = with_ends(jax.random.randint(streams_of[1], (QUERIES,), 0, CTX), jax.random.fold_in(streams_of[1], 1), 0, CTX - 1).astype(jnp.int32)
    query_feat = with_ends(jax.random.randint(streams_of[2], (QUERIES,), 0, NMON), jax.random.fold_in(streams_of[2], 1), 0, NMON - 1).astype(jnp.int32)
    sae_enc = noise(streams_of[3], (NMON, DOUT), 1.0, 6.0, ((1, 8),))
    basis_in = noise(streams_of[4], (DIN, DIN), DIN ** -0.5, 0.078125, ((0, 32), (1, 8)))
    basis_out = noise(streams_of[5], (DOUT, DOUT), DOUT ** -0.5, 0.0390625, ((0, 8), (1, 32)))
    eigvals = draw_eigvals(jax.random.fold_in(streams_of[9], 71), 0)
    train_in = noise(streams_of[7], (SEQS, R, DIN), 1.0, 6.0, ((0, 32), (2, 8)))
    train_out = noise(streams_of[8], (SEQS, R, DOUT), 1.0, 6.0, ((0, 32),))
    return dict(query_acts=query_acts, query_pos=query_pos, query_feat=query_feat, sae_enc=sae_enc, basis_in=basis_in, basis_out=basis_out, eigvals=eigvals, train_in=train_in, train_out=train_out)


damping = 0.1

def reference(query_acts, query_pos, query_feat, sae_enc, basis_in, basis_out, eigvals, train_in, train_out):
    inputs = query_acts[query_pos]
    outputs = sae_enc[query_feat]
    a_eig = jnp.dot(inputs, basis_in, preferred_element_type=jnp.float32)
    b_eig = jnp.dot(outputs, basis_out, preferred_element_type=jnp.float32).astype(jnp.bfloat16)
    mean_eig = jnp.sum(eigvals) / (DIN * DOUT)
    inverse = 1.0 / (eigvals + damping * mean_eig)
    b_wide = b_eig.astype(jnp.float32)

    def one_seq(pair):
        left, right = pair
        cross = jnp.dot(left.astype(jnp.float32).T, right.astype(jnp.float32), precision=lax.Precision.HIGHEST)
        damped = (cross * inverse).astype(jnp.bfloat16)
        projected = jnp.dot(damped.astype(jnp.float32), b_wide.T, precision=lax.Precision.HIGHEST)
        return lax.optimization_barrier(jnp.sum(a_eig.T * projected, axis=0))
    scores = lax.map(one_seq, (train_in, train_out))
    return scores.T / math.sqrt(DIN * DOUT * R)
```

```python
import math

import jax
import jax.numpy as jnp
from jax import lax
from jax.experimental import pallas as pl
from jax.experimental.pallas import tpu as pltpu
from jax.sharding import PartitionSpec as P

DIN = 5120
DOUT = 27648
R = 32
damping = 0.1

ZH, X, CORE, Y, ZL = 4, 4, 2, 4, 2
XC = X * CORE
DP = ZH * XC
TENSOR = Y * ZL
SEQS = 32
Q = 64
I = DIN // TENSOR
J = DOUT // DP
JP = 1024
MESH = pl.DeviceIdType.MESH
f32 = jnp.float32
bf16 = jnp.bfloat16
FIRST_ROWS = (((0,), (0,)), ((), ()))


def kernel(
    pos_ref, feat_ref, acts_hbm, sae_hbm, bin_hbm, bout_hbm, eig_hbm, tin_hbm, tout_hbm,
    out_ref,
    acts, sae, bin_, bout, eig, tout, inv, right_out, right, left,
    b_part, b_recv, b_sum, b_all, b_lo,
    e_sum, e_xc, e_mid, e_z,
    a_part, a_xc, a_mid, a_z, a_sum, a_all, a_full,
    damped, scores, f_part, f_z, f_mid, f_xc, f_last, f_t,
    local_sem, r_send, r_recv, y_send, y_again, lz_send, lz_recv, lx_send, lx_recv, lc_send, lc_recv,
    b_send, b_rsem, bg_send, bg_recv, e_send, e_recv, ez_send, ez_recv,
    a_send, a_recv, az_send, az_recv, ag_send, ag_recv,
    fz_send, fz_recv, fx_send, fx_recv, ft_send, ft_recv,
):
    d = lax.axis_index("dp")
    t = lax.axis_index("tensor")
    zh, xc = lax.div(d, XC), lax.rem(d, XC)
    x, core = lax.div(xc, CORE), lax.rem(xc, CORE)
    y, zl = lax.div(t, ZL), lax.rem(t, ZL)

    def remote(src, dst, send, recv, dp, tensor):
        return pltpu.make_async_remote_copy(
            src_ref=src, dst_ref=dst, send_sem=send, recv_sem=recv,
            device_id={"dp": dp, "tensor": tensor}, device_id_type=MESH,
        )

    def others(count, me, body):
        def step(k, carry):
            body(lax.rem(me + k, count))
            return carry

        lax.fori_loop(1, count, step, 0)

    def spread(count, me, src, dst, send, recv, place):
        def body(o):
            dp, tensor = place(o)
            remote(src(o), dst.at[me], send.at[o], recv.at[me], dp, tensor).start()

        others(count, me, body)

    def collect(count, me, src, dst, send, recv):
        def body(o):
            remote(src(o), dst.at[o], send.at[o], recv.at[o], d, t).wait_recv()

        others(count, me, body)

    def drain(count, me, src, dst, send, recv):
        def body(o):
            remote(src(o), dst.at[me], send.at[o], recv.at[me], d, t).wait_send()

        others(count, me, body)

    in_xc = lambda o: (zh * XC + o, t)
    in_zh = lambda o: (o * XC + xc, t)
    in_t = lambda o: (d, o)
    in_dp = lambda o: (o, t)

    loads = [
        pltpu.make_async_copy(src, dst, local_sem.at[n])
        for n, (src, dst) in enumerate((
            (tout_hbm, tout), (tin_hbm, left.at[zh, x, core]), (eig_hbm, eig), (sae_hbm, sae),
            (bout_hbm, bout), (acts_hbm, acts), (bin_hbm, bin_),
        ))
    ]
    for load in loads:
        load.start()
    l_tout, l_tin, l_eig, l_sae, l_bout, l_acts, l_bin = loads

    barrier = pltpu.get_barrier_semaphore()

    def greet_dp(o):
        pl.semaphore_signal(barrier, inc=1, device_id={"dp": o, "tensor": t}, device_id_type=MESH)

    def greet_t(o):
        pl.semaphore_signal(barrier, inc=1, device_id={"dp": d, "tensor": o}, device_id_type=MESH)

    others(DP, d, greet_dp)
    others(TENSOR, t, greet_t)

    is_source = lax.rem(x + zh + 2 * core + zl, Y) == y

    l_tout.wait()

    @pl.when(is_source)
    def _():
        def four(g, carry):
            wide = tout[:, pl.ds(pl.multiple_of(g * (4 * J), 128), 4 * J)]
            for p in range(4):
                right_out[g * 4 + p] = wide[:, p * J:(p + 1) * J]
            return carry

        lax.fori_loop(0, DP // 4, four, 0)

    l_tin.wait()
    pl.semaphore_wait(barrier, DP + TENSOR - 2)

    def left_z(o):
        remote(left.at[zh, x, core], left.at[zh, x, core], lz_send.at[o], lz_recv.at[zh],
               o * XC + xc, t).start()

    others(ZH, zh, left_z)

    @pl.when(is_source)
    def _():
        pltpu.make_async_copy(right_out.at[d], right.at[d], r_recv.at[d]).start()

        def send(o):
            remote(right_out.at[o], right.at[d], r_send.at[o], r_recv.at[d], o, t).start()

        others(DP, d, send)

    l_eig.wait()
    folded = jnp.sum(eig[...].reshape(I // 8, 8, J), axis=0)
    e_part = jnp.concatenate([folded[:, 768:], jnp.zeros((8, 32), f32)], axis=1)
    for n in range(6):
        e_part = e_part + folded[:, n * 128:(n + 1) * 128]

    l_sae.wait()
    monitored = sae.shape[0]
    chooser = jnp.where(
        lax.broadcasted_iota(jnp.int32, (monitored, Q), 0) == feat_ref[...], 1.0, 0.0
    ).astype(bf16)
    outputs = lax.dot_general(chooser, sae[...], FIRST_ROWS, preferred_element_type=f32).astype(bf16)
    l_bout.wait()
    b_mine = jnp.dot(outputs, bout[...], preferred_element_type=f32)
    for n in range(TENSOR):
        b_part[n, :, 0:J] = b_mine[8 * n:8 * (n + 1)]
        b_part[n, :, 896:JP] = e_part
    spread(TENSOR, t, lambda o: b_part.at[o], b_recv, b_send, b_rsem, in_t)
    b_recv[t] = b_part[t]

    def left_z_wait(o):
        remote(left.at[o, x, core], left.at[o, x, core], lz_send.at[o], lz_recv.at[o], d, t).wait_recv()

    others(ZH, zh, left_z_wait)

    def left_x(o):
        remote(left.at[:, x, core], left.at[:, x, core], lx_send.at[o], lx_recv.at[x],
               zh * XC + o * CORE + core, t).start()

    others(X, x, left_x)

    def left_core(o):
        remote(left.at[:, o, core], left.at[:, o, core], lc_send.at[o], lc_recv.at[o],
               zh * XC + x * CORE + (1 - core), t).start()

    left_core(x)

    l_acts.wait()
    context = acts.shape[0]
    picker = jnp.where(
        lax.broadcasted_iota(jnp.int32, (context, Q), 0) == pos_ref[...], 1.0, 0.0
    ).astype(bf16)
    inputs = lax.dot_general(picker, acts[...], FIRST_ROWS, preferred_element_type=f32).astype(bf16)
    l_bin.wait()
    a_mine = jnp.dot(inputs, bin_[...], preferred_element_type=f32)
    for n in range(XC):
        a_part[n] = a_mine[8 * n:8 * (n + 1)]
    spread(XC, xc, lambda o: a_part.at[o], a_xc, a_send, a_recv, in_xc)
    a_xc[xc] = a_part[xc]

    collect(TENSOR, t, lambda o: b_part.at[o], b_recv, b_send, b_rsem)
    total = b_recv[0]
    for n in range(1, TENSOR):
        total = total + b_recv[n]
    b_sum[...] = total[:, 0:896]
    e_sum[...] = total[:, 896:JP]
    spread(XC, xc, lambda o: e_sum, e_xc, e_send, e_recv, in_xc)
    spread(TENSOR, t, lambda o: b_sum, b_all, bg_send, bg_recv, in_t)
    e_xc[xc] = e_sum[...]
    b_all[t] = b_sum[...]

    for n in range(I // 128):
        inv[:, n * 128:(n + 1) * 128] = eig[n * 128:(n + 1) * 128, :].T

    def left_x_wait(o):
        remote(left.at[:, o, core], left.at[:, o, core], lx_send.at[o], lx_recv.at[o], d, t).wait_recv()
        left_core(o)

    others(X, x, left_x_wait)

    collect(XC, xc, lambda o: e_sum, e_xc, e_send, e_recv)
    total = e_xc[0]
    for n in range(1, XC):
        total = total + e_xc[n]
    e_mid[...] = total
    spread(ZH, zh, lambda o: e_mid, e_z, ez_send, ez_recv, in_zh)
    e_z[zh] = e_mid[...]

    collect(XC, xc, lambda o: a_part.at[o], a_xc, a_send, a_recv)
    total = a_xc[0]
    for n in range(1, XC):
        total = total + a_xc[n]
    a_mid[...] = total
    spread(ZH, zh, lambda o: a_mid, a_z, az_send, az_recv, in_zh)
    a_z[zh] = a_mid[...]

    collect(TENSOR, t, lambda o: b_sum, b_all, bg_send, bg_recv)
    for n in range(TENSOR // 2):
        pair = jnp.concatenate([b_all[2 * n], b_all[2 * n + 1]], axis=0)
        b_lo[16 * n:16 * (n + 1), :] = pair.astype(bf16)[:, 0:J]

    collect(ZH, zh, lambda o: a_mid, a_z, az_send, az_recv)
    a_sum[...] = ((a_z[0] + a_z[1]) + (a_z[2] + a_z[3])) * (1.0 / math.sqrt(DIN * DOUT * R))
    spread(XC, xc, lambda o: a_sum, a_all, ag_send, ag_recv, in_xc)
    a_all[xc] = a_sum[...]

    collect(ZH, zh, lambda o: e_mid, e_z, ez_send, ez_recv)
    eig_total = jnp.sum((e_z[0] + e_z[1]) + (e_z[2] + e_z[3]))
    shift = damping * (eig_total / (DIN * DOUT))

    def invert(n, carry):
        rows = pl.ds(pl.multiple_of(n * 96, 8), 96)
        inv[rows, :] = 1.0 / (inv[rows, :] + shift)
        return carry

    lax.fori_loop(0, J // 96, invert, 0)

    def seq_of(k):
        g, m = lax.div(k, 8), lax.rem(k, 8)
        low = m < 4
        off = jnp.where(g == 0, 0, jnp.where(g == 3, 2, jnp.where((g == 1) == low, 1, 3)))
        plane = lax.rem(y + off, Y)
        sz, sc = lax.div(m, CORE), lax.rem(m, CORE)
        sx = lax.rem(plane - sz - 2 * sc - zl + 2 * Y, Y)
        return sz, sx, sc

    def flat(s):
        return (s[0] * X + s[1]) * CORE + s[2]

    def right_wait(s):
        remote(right.at[s], right.at[s], y_again.at[0], r_recv.at[s], d, t).wait_recv()

    def to_plane(s, off, sem):
        return remote(right.at[s], right.at[s], sem, r_recv.at[s], d, lax.rem(y + off, Y) * ZL + zl)

    def own(m, carry):
        s = flat(seq_of(m))
        right_wait(s)
        to_plane(s, 1, y_send.at[0, m]).start()
        to_plane(s, 3, y_send.at[1, m]).start()
        return carry

    lax.fori_loop(0, 8, own, 0)

    def left_core_wait(o, carry):
        remote(left.at[:, o, 1 - core], left.at[:, o, 1 - core], lc_send.at[o], lc_recv.at[o], d, t).wait_recv()
        return carry

    lax.fori_loop(0, X, left_core_wait, 0)

    collect(XC, xc, lambda o: a_sum, a_all, ag_send, ag_recv)
    for n in range(XC):
        a_full[8 * n:8 * (n + 1), :] = a_all[n]

    def ready(k):
        @pl.when(k >= 8)
        def _():
            s = flat(seq_of(k))
            right_wait(s)

            @pl.when(k < 16)
            def _():
                m = k - 8
                to_plane(s, jnp.where(m < 4, 3, 1), y_again.at[m]).start()

    def cross(k, slot):
        s = seq_of(k)
        wide = lax.dot_general(
            right[flat(s)], left[s[0], s[1], s[2]], FIRST_ROWS, preferred_element_type=f32
        )
        damped[slot] = (wide * inv[...]).astype(bf16)

    def project(k, slot):
        s = flat(seq_of(k))
        part = jnp.dot(b_lo[...], damped[slot], preferred_element_type=f32) * a_full[...]
        row = part[:, 0:128]
        for n in range(1, I // 128):
            row = row + part[:, n * 128:(n + 1) * 128]
        row = jnp.sum(row, axis=1, keepdims=True)
        lane = lax.broadcasted_iota(jnp.int32, (Q, 128), 1)
        scores[...] = jnp.where(lane == s, row, scores[...])

    scores[...] = jnp.zeros_like(scores)
    cross(0, 0)

    def two(h, carry):
        k = 2 * h
        ready(k + 1)
        cross(k + 1, 1)
        project(k, 0)
        ready(k + 2)
        cross(k + 2, 0)
        project(k + 1, 1)
        return carry

    lax.fori_loop(0, SEQS // 2 - 1, two, 0)
    ready(SEQS - 1)
    cross(SEQS - 1, 1)
    project(SEQS - 2, 0)
    project(SEQS - 1, 1)

    rows = scores[...].T
    for n in range(ZH):
        f_part[n, :, 0:Q] = rows[8 * n:8 * (n + 1), :]
        f_part[n, :, Q:128] = jnp.zeros((8, 128 - Q), f32)
    spread(ZH, zh, lambda o: f_part.at[o], f_z, fz_send, fz_recv, in_zh)
    f_z[zh] = f_part[zh]
    collect(ZH, zh, lambda o: f_part.at[o], f_z, fz_send, fz_recv)
    f_mid[...] = (f_z[0] + f_z[1]) + (f_z[2] + f_z[3])
    spread(XC, xc, lambda o: f_mid, f_xc, fx_send, fx_recv, in_xc)
    f_xc[xc] = f_mid[...]
    collect(XC, xc, lambda o: f_mid, f_xc, fx_send, fx_recv)
    total = f_xc[0]
    for n in range(1, XC):
        total = total + f_xc[n]
    f_last[...] = total
    spread(TENSOR, t, lambda o: f_last, f_t, ft_send, ft_recv, in_t)
    f_t[t] = f_last[...]

    @pl.when(is_source)
    def _():
        def sent(o):
            remote(right_out.at[o], right.at[d], r_send.at[o], r_recv.at[d], o, t).wait_send()

        others(DP, d, sent)

    def sent_y(m, carry):
        to_plane(0, 1, y_send.at[0, m]).wait_send()
        to_plane(0, 1, y_send.at[1, m]).wait_send()
        to_plane(0, 1, y_again.at[m]).wait_send()
        return carry

    lax.fori_loop(0, 8, sent_y, 0)
    drain(TENSOR, t, lambda o: b_part.at[o], b_recv, b_send, b_rsem)
    drain(TENSOR, t, lambda o: b_sum, b_all, bg_send, bg_recv)
    drain(XC, xc, lambda o: e_sum, e_xc, e_send, e_recv)
    drain(ZH, zh, lambda o: e_mid, e_z, ez_send, ez_recv)
    drain(XC, xc, lambda o: a_part.at[o], a_xc, a_send, a_recv)
    drain(ZH, zh, lambda o: a_mid, a_z, az_send, az_recv)
    drain(XC, xc, lambda o: a_sum, a_all, ag_send, ag_recv)
    drain(ZH, zh, lambda o: f_part.at[o], f_z, fz_send, fz_recv)
    drain(XC, xc, lambda o: f_mid, f_xc, fx_send, fx_recv)

    def sent_left_z(o):
        remote(left.at[zh, x, core], left.at[zh, x, core], lz_send.at[o], lz_recv.at[zh], d, t).wait_send()

    others(ZH, zh, sent_left_z)

    def sent_left_x(o):
        remote(left.at[:, x, core], left.at[:, x, core], lx_send.at[o], lx_recv.at[x], d, t).wait_send()

    others(X, x, sent_left_x)

    def sent_left_core(o, carry):
        remote(left.at[:, o, core], left.at[:, o, core], lc_send.at[o], lc_recv.at[o], d, t).wait_send()
        return carry

    lax.fori_loop(0, X, sent_left_core, 0)

    collect(TENSOR, t, lambda o: f_last, f_t, ft_send, ft_recv)
    total = f_t[0]
    for n in range(1, TENSOR):
        total = total + f_t[n]
    f_last_row = jnp.sum(
        jnp.where(lax.broadcasted_iota(jnp.int32, (8, 128), 0) == xc, total, 0.0), axis=0, keepdims=True
    )
    out_ref[...] = jnp.broadcast_to(f_last_row, (8, 128)).T[0:Q, 0:1]
    drain(TENSOR, t, lambda o: f_last, f_t, ft_send, ft_recv)


def on_device(
    query_acts, query_pos, query_feat, sae_enc, basis_in, basis_out, eigvals, train_in, train_out
):
    context = query_acts.shape[0]
    monitored = sae_enc.shape[0]
    vmem = pltpu.VMEM
    dma = pltpu.SemaphoreType.DMA
    scratch = [
        vmem((context, DIN // DP), bf16), vmem((monitored, DOUT // TENSOR), bf16),
        vmem((DIN // DP, I), bf16), vmem((DOUT // TENSOR, J), bf16), vmem((I, J), f32),
        vmem((R, DOUT), bf16), vmem((J, I), f32),
        vmem((DP, R, J), bf16), vmem((SEQS, R, J), bf16), vmem((ZH, X, CORE, R, I), bf16),
        vmem((TENSOR, 8, JP), f32), vmem((TENSOR, 8, JP), f32), vmem((8, 896), f32),
        vmem((TENSOR, 8, 896), f32), vmem((Q, J), bf16),
        vmem((8, 128), f32), vmem((XC, 8, 128), f32), vmem((8, 128), f32), vmem((ZH, 8, 128), f32),
        vmem((XC, 8, I), f32), vmem((XC, 8, I), f32), vmem((8, I), f32), vmem((ZH, 8, I), f32),
        vmem((8, I), f32), vmem((XC, 8, I), f32), vmem((Q, I), f32),
        vmem((2, J, I), bf16), vmem((Q, 128), f32),
        vmem((ZH, 8, 128), f32), vmem((ZH, 8, 128), f32), vmem((8, 128), f32),
        vmem((XC, 8, 128), f32), vmem((8, 128), f32), vmem((TENSOR, 8, 128), f32),
        dma((7,)), dma((DP,)), dma((SEQS,)), dma((2, 8)), dma((8,)),
        dma((ZH,)), dma((ZH,)), dma((X,)), dma((X,)), dma((X,)), dma((X,)),
        dma((TENSOR,)), dma((TENSOR,)), dma((TENSOR,)), dma((TENSOR,)),
        dma((XC,)), dma((XC,)), dma((ZH,)), dma((ZH,)),
        dma((XC,)), dma((XC,)), dma((ZH,)), dma((ZH,)), dma((XC,)), dma((XC,)),
        dma((ZH,)), dma((ZH,)), dma((XC,)), dma((XC,)), dma((TENSOR,)), dma((TENSOR,)),
    ]
    anywhere = pl.BlockSpec(memory_space=pl.ANY)
    inside = pl.BlockSpec(memory_space=pltpu.VMEM)
    return pl.pallas_call(
        kernel,
        out_shape=jax.ShapeDtypeStruct((Q, 1), f32),
        in_specs=[inside, inside] + [anywhere] * 7,
        out_specs=inside,
        scratch_shapes=scratch,
        compiler_params=pltpu.CompilerParams(
            collective_id=0, has_side_effects=True, vmem_limit_bytes=56 << 20
        ),
        name="influence",
    )(
        query_pos.reshape(1, Q), query_feat.reshape(1, Q), query_acts, sae_enc, basis_in, basis_out,
        eigvals, train_in.reshape(R, I), train_out.reshape(R, DOUT),
    )


def solution(mesh):
    in_specs = (
        P(None, "dp"),
        P(),
        P(),
        P(None, "tensor"),
        P("dp", "tensor"),
        P("tensor", "dp"),
        P("tensor", "dp"),
        P("dp", None, "tensor"),
        P("dp", None, None),
    )
    out_specs = P(None, "dp")
    return jax.shard_map(
        on_device, mesh=mesh, in_specs=in_specs, out_specs=out_specs, check_vma=False
    )
```

```python
import math

import jax
import jax.numpy as jnp
from jax import lax
from jax.experimental import pallas as pl
from jax.experimental.pallas import tpu as pltpu
from jax.sharding import PartitionSpec as P

DIN = 5120
DOUT = 27648
R = 32
damping = 0.1

ZH, X, CORE, Y, ZL = 4, 4, 2, 4, 2
XC = X * CORE
DP = ZH * XC
TENSOR = Y * ZL
SEQS = 32
Q = 64
I = DIN // TENSOR
J = DOUT // DP
JP = 896
MESH = pl.DeviceIdType.MESH
f32 = jnp.float32
bf16 = jnp.bfloat16
FIRST_ROWS = (((0,), (0,)), ((), ()))
LAST_COLUMNS = (((1,), (1,)), ((), ()))


def wrap(v, n):
    return jnp.where(v >= n, v - n, v)


def half_of(v):
    return jnp.where(v >= 4, jnp.where(v >= 6, 3, 2), jnp.where(v >= 2, 1, 0))


def kernel(
    pos_ref, feat_ref, acts_hbm, sae_hbm, bin_hbm, bout_hbm, eig_hbm, tin_hbm, tout_hbm,
    out_ref,
    acts, sae, bin_, bout, inv, tout, right_out, right_row, right, left,
    b_mine, b_part, b_recv, b_sum, b_all, b_lo,
    e_mine, e_z, e_sum, e_xc, e_mid, e_t,
    a_part, a_xc, a_mid, a_z, a_sum, a_all, a_full,
    damped, rows, scores, f_part, f_z, f_mid, f_xc, f_last, f_t,
    local_sem, rz_send, rz_recv, r_send, r_recv, y_send, y_again, lz_send, lz_recv, lx_send, lx_recv, lc_send, lc_recv,
    b_send, b_rsem, bg_send, bg_recv, ez_send, ez_recv, e_send, e_recv, et_send, et_recv,
    a_send, a_recv, az_send, az_recv, ag_send, ag_recv,
    fz_send, fz_recv, fx_send, fx_recv, ft_send, ft_recv,
):
    d = lax.axis_index("dp")
    t = lax.axis_index("tensor")
    zh, xc = lax.div(d, XC), lax.rem(d, XC)
    x, core = lax.div(xc, CORE), lax.rem(xc, CORE)
    y, zl = lax.div(t, ZL), lax.rem(t, ZL)

    def remote(src, dst, send, recv, dp, tensor):
        return pltpu.make_async_remote_copy(
            src_ref=src, dst_ref=dst, send_sem=send, recv_sem=recv,
            device_id={"dp": dp, "tensor": tensor}, device_id_type=MESH,
        )

    def total_of(ref, count):
        total = ref[0]
        for n in range(1, count):
            total = total + ref[n]
        return total

    def others(count, me, body):
        def step(k, carry):
            body(wrap(me + k, count))
            return carry

        lax.fori_loop(1, count, step, 0)

    def spread(count, me, src, dst, send, recv, place):
        def body(o):
            dp, tensor = place(o)
            remote(src(o), dst.at[me], send.at[o], recv.at[me], dp, tensor).start()

        others(count, me, body)

    def collect(count, me, src, dst, send, recv):
        def body(o):
            remote(src(o), dst.at[o], send.at[o], recv.at[o], d, t).wait_recv()

        others(count, me, body)

    def drain(count, me, src, dst, send, recv):
        def body(o):
            remote(src(o), dst.at[me], send.at[o], recv.at[me], d, t).wait_send()

        others(count, me, body)

    in_xc = lambda o: (zh * XC + o, t)
    in_zh = lambda o: (o * XC + xc, t)
    in_t = lambda o: (d, o)

    loads = [
        pltpu.make_async_copy(src, dst, local_sem.at[n])
        for n, (src, dst) in enumerate((
            (tout_hbm, tout), (tin_hbm, left.at[zh, x, core]), (eig_hbm, inv), (acts_hbm, acts), (bin_hbm, bin_),
            (sae_hbm, sae), (bout_hbm, bout),
        ))
    ]
    for load in loads:
        load.start()
    l_tout, l_tin, l_eig, l_acts, l_bin, l_sae, l_bout = loads

    barrier = pltpu.get_barrier_semaphore()

    def greet(place):
        def body(o):
            dp, tensor = place(o)
            pl.semaphore_signal(barrier, inc=1, device_id={"dp": dp, "tensor": tensor}, device_id_type=MESH)

        return body

    others(ZH, zh, greet(in_zh))
    others(TENSOR, t, greet(in_t))
    others(XC, xc, greet(in_xc))

    def low_two(v):
        return wrap(wrap(v, 8), 4)

    hop = low_two(x + 2 * core + zl - y + Y)
    row = wrap(zh + hop, ZH)
    column_seq = wrap(zh - hop + ZH, ZH) * XC + xc

    l_tout.wait()

    def four(half, carry):
        wide = tout[:, pl.ds(pl.multiple_of((2 * row + half) * (4 * J), 128), 4 * J)]
        for p in range(4):
            right_out[half * 4 + p, :, 0:J] = wide[:, p * J:(p + 1) * J]
        return carry

    lax.fori_loop(0, 2, four, 0)

    l_eig.wait()

    def fold(n, total):
        some = inv[pl.ds(pl.multiple_of(n * 96, 8), 96), :]
        some = jnp.sum(some.reshape(12, 8, I), axis=0)
        for c in range(I // 128):
            total = total + some[:, c * 128:(c + 1) * 128]
        return total

    e_part = lax.fori_loop(0, J // 96, fold, jnp.zeros((8, 128), f32))
    e_mine[...] = e_part
    e_z[zh] = e_part
    l_tin.wait()

    pl.semaphore_wait(barrier, ZH + TENSOR + XC - 3)
    spread(ZH, zh, lambda o: e_mine, e_z, ez_send, ez_recv, in_zh)

    def left_z(o):
        return remote(left.at[zh, x, core], left.at[zh, x, core], lz_send.at[o], lz_recv.at[zh],
                      o * XC + xc, t)

    others(ZH, zh, lambda o: left_z(o).start())

    def right_z(quarter):
        blocks = pl.ds(wrap(x + quarter, X) * CORE, CORE)
        return remote(right_out.at[blocks], right_row.at[blocks], rz_send.at[quarter], rz_recv.at[quarter],
                      row * XC + xc, t)

    @pl.when(hop != 0)
    def _():
        lax.fori_loop(0, X, lambda quarter, carry: (right_z(quarter).start(), carry)[1], 0)

    @pl.when(hop == 0)
    def _():
        def here(quarter, carry):
            blocks = pl.ds(wrap(x + quarter, X) * CORE, CORE)
            pltpu.make_async_copy(right_out.at[blocks], right_row.at[blocks], rz_recv.at[quarter]).start()
            return carry

        lax.fori_loop(0, X, here, 0)

    l_sae.wait()
    monitored = sae.shape[0]
    chooser = jnp.where(
        lax.broadcasted_iota(jnp.int32, (monitored, Q), 0) == feat_ref[...], 1.0, 0.0
    ).astype(bf16)
    l_bout.wait()
    wide = 384
    b_mine[...] = jnp.zeros_like(b_mine)

    def b_step(n, carry):
        columns = pl.ds(pl.multiple_of(n * wide, 128), wide)
        outputs = lax.dot_general(
            chooser, sae[:, columns], FIRST_ROWS, preferred_element_type=f32
        ).astype(bf16)
        b_mine[...] += lax.dot_general(
            outputs, bout[:, columns], LAST_COLUMNS, preferred_element_type=f32
        )
        return carry

    lax.fori_loop(0, DOUT // TENSOR // wide, b_step, 0)
    for n in range(TENSOR):
        b_part[n, :, 0:J] = b_mine[8 * n:8 * (n + 1), :]
    spread(TENSOR, t, lambda o: b_part.at[o], b_recv, b_send, b_rsem, in_t)
    b_recv[t] = b_part[t]

    l_acts.wait()
    context = acts.shape[1]
    picker = jnp.where(
        lax.broadcasted_iota(jnp.int32, (context, Q), 0) == pos_ref[...], 1.0, 0.0
    ).astype(bf16)
    inputs = jnp.dot(acts[...], picker, preferred_element_type=f32).astype(bf16)
    l_bin.wait()
    a_mine = lax.dot_general(inputs, bin_[...], FIRST_ROWS, preferred_element_type=f32)
    for n in range(XC):
        a_part[n] = a_mine[8 * n:8 * (n + 1)]
    spread(XC, xc, lambda o: a_part.at[o], a_xc, a_send, a_recv, in_xc)
    a_xc[xc] = a_part[xc]

    collect(ZH, zh, lambda o: e_mine, e_z, ez_send, ez_recv)
    e_sum[...] = total_of(e_z, ZH)
    spread(XC, xc, lambda o: e_sum, e_xc, e_send, e_recv, in_xc)
    e_xc[xc] = e_sum[...]

    def left_x(o):
        return remote(left.at[:, x, core], left.at[:, x, core], lx_send.at[o], lx_recv.at[x],
                      zh * XC + o * CORE + core, t)

    def left_core(o):
        return remote(left.at[:, o, core], left.at[:, o, core], lc_send.at[o], lc_recv.at[o],
                      zh * XC + x * CORE + (1 - core), t)

    others(ZH, zh, lambda o: remote(
        left.at[o, x, core], left.at[o, x, core], lz_send.at[o], lz_recv.at[o], d, t).wait_recv())
    others(X, x, lambda o: left_x(o).start())
    left_core(x).start()

    def right_x(o):
        return remote(right_row.at[o], right.at[column_seq], r_send.at[o], r_recv.at[column_seq],
                      zh * XC + o, t)

    def right_quarter(quarter):
        right_z(quarter).wait_recv()

        def one(c, carry):
            o = wrap(x + quarter, X) * CORE + c

            @pl.when(o != xc)
            def _():
                right_x(o).start()

            @pl.when(o == xc)
            def _():
                pltpu.make_async_copy(right_row.at[o], right.at[column_seq], r_recv.at[column_seq]).start()

            return carry

        lax.fori_loop(0, CORE, one, 0)

    def seq_of(k):
        g = jnp.where(k >= 16, jnp.where(k >= 24, 3, 2), jnp.where(k >= 8, 1, 0))
        m = k - 8 * g
        off = jnp.where(g == 0, 0, jnp.where(g == 3, 2, jnp.where((g == 1) == (m < 4), 1, 3)))
        pair = half_of(m)
        sx, sc = wrap(x - pair + X, X), m - 2 * pair
        return low_two(zh + wrap(y + off, Y) - sx - 2 * sc - zl + 2 * Y), sx, sc

    def flat(s):
        return (s[0] * X + s[1]) * CORE + s[2]

    def right_wait(s):
        remote(right.at[s], right.at[s], y_again.at[0], r_recv.at[s], d, t).wait_recv()

    def to_plane(s, off, sem):
        return remote(right.at[s], right.at[s], sem, r_recv.at[s], d, wrap(y + off, Y) * ZL + zl)

    def own(m, carry):
        s = flat(seq_of(m))
        right_wait(s)
        to_plane(s, 1, y_send.at[0, m]).start()
        to_plane(s, 3, y_send.at[1, m]).start()
        return carry

    right_quarter(0)
    right_quarter(1)

    collect(XC, xc, lambda o: a_part.at[o], a_xc, a_send, a_recv)
    a_mid[...] = total_of(a_xc, XC)
    spread(ZH, zh, lambda o: a_mid, a_z, az_send, az_recv, in_zh)
    a_z[zh] = a_mid[...]

    collect(TENSOR, t, lambda o: b_part.at[o], b_recv, b_send, b_rsem)
    b_sum[...] = total_of(b_recv, TENSOR)
    spread(TENSOR, t, lambda o: b_sum, b_all, bg_send, bg_recv, in_t)
    b_all[t] = b_sum[...]

    lax.fori_loop(0, 2, own, 0)
    right_quarter(2)

    collect(XC, xc, lambda o: e_sum, e_xc, e_send, e_recv)
    e_mid[...] = total_of(e_xc, XC)
    spread(TENSOR, t, lambda o: e_mid, e_t, et_send, et_recv, in_t)
    e_t[t] = e_mid[...]

    lax.fori_loop(2, 4, own, 0)
    right_quarter(3)

    collect(ZH, zh, lambda o: a_mid, a_z, az_send, az_recv)
    a_sum[...] = total_of(a_z, ZH) * (1.0 / math.sqrt(DIN * DOUT * R))
    spread(XC, xc, lambda o: a_sum, a_all, ag_send, ag_recv, in_xc)
    a_all[xc] = a_sum[...]

    def left_x_wait(o):
        remote(left.at[:, o, core], left.at[:, o, core], lx_send.at[o], lx_recv.at[o], d, t).wait_recv()
        left_core(o).start()

    others(X, x, left_x_wait)
    lax.fori_loop(4, 6, own, 0)

    collect(TENSOR, t, lambda o: e_mid, e_t, et_send, et_recv)
    shift = damping * (jnp.sum(total_of(e_t, TENSOR)) / (DIN * DOUT))

    def invert(n, carry):
        some = pl.ds(pl.multiple_of(n * 96, 8), 96)
        inv[some, :] = 1.0 / (inv[some, :] + shift)
        return carry

    lax.fori_loop(0, J // 96, invert, 0)

    collect(TENSOR, t, lambda o: b_sum, b_all, bg_send, bg_recv)
    for n in range(TENSOR // 2):
        pair = jnp.concatenate([b_all[2 * n], b_all[2 * n + 1]], axis=0)
        b_lo[16 * n:16 * (n + 1), :] = pair.astype(bf16)[:, 0:J]

    lax.fori_loop(6, 8, own, 0)

    def left_core_wait(o, carry):
        remote(left.at[:, o, 1 - core], left.at[:, o, 1 - core], lc_send.at[o], lc_recv.at[o], d, t).wait_recv()
        return carry

    lax.fori_loop(0, X, left_core_wait, 0)

    collect(XC, xc, lambda o: a_sum, a_all, ag_send, ag_recv)
    for n in range(XC):
        a_full[8 * n:8 * (n + 1), :] = a_all[n]

    def ready(part):
        def arrived(k, carry):
            right_wait(flat(seq_of(k)))
            return carry

        def arrived_and_on(k, carry):
            s = flat(seq_of(k))
            right_wait(s)
            m = k - 8
            to_plane(s, jnp.where(m < 4, 3, 1), y_again.at[m]).start()
            return carry

        first = part * 4

        @pl.when(jnp.logical_and(part >= 2, part < 4))
        def _():
            lax.fori_loop(first, first + 4, arrived_and_on, 0)

        @pl.when(part >= 4)
        def _():
            lax.fori_loop(first, first + 4, arrived, 0)

    def cross(s, slot):
        wide = lax.dot_general(
            right[flat(s), :, 0:J], left[s[0], s[1], s[2]], FIRST_ROWS, preferred_element_type=f32
        )
        damped[slot] = (wide * inv[...]).astype(bf16)

    def project(slot):
        part = jnp.dot(b_lo[...], damped[slot], preferred_element_type=f32) * a_full[...]
        row = part[:, 0:128]
        for n in range(1, I // 128):
            row = row + part[:, n * 128:(n + 1) * 128]
        rows[slot] = row

    def score(of, slot):
        row = jnp.sum(rows[slot], axis=1, keepdims=True)
        lane = lax.broadcasted_iota(jnp.int32, (Q, 128), 1)
        scores[...] = jnp.where(lane == of, row, scores[...])

    def step(k, before, slot):
        s = seq_of(k)
        cross(s, slot)
        project(1 - slot)
        score(before[0], slot)
        return before[1], flat(s)

    scores[...] = jnp.zeros_like(scores)
    rows[...] = jnp.zeros_like(rows)
    damped[1] = jnp.zeros((J, I), bf16)

    def eighth(part, before):
        ready(part)

        def two(h, before):
            before = step(part * 4 + 2 * h, before, 0)
            return step(part * 4 + 2 * h + 1, before, 1)

        return lax.fori_loop(0, 2, two, before)

    before = lax.fori_loop(0, SEQS // 4, eighth, (-1, -1))
    project(1)
    score(before[0], 0)
    score(before[1], 1)

    by_seq = scores[...].T
    for n in range(ZH):
        f_part[n, :, 0:Q] = by_seq[8 * n:8 * (n + 1), :]
        f_part[n, :, Q:128] = jnp.zeros((8, 128 - Q), f32)
    spread(ZH, zh, lambda o: f_part.at[o], f_z, fz_send, fz_recv, in_zh)
    f_z[zh] = f_part[zh]
    collect(ZH, zh, lambda o: f_part.at[o], f_z, fz_send, fz_recv)
    f_mid[...] = (f_z[0] + f_z[1]) + (f_z[2] + f_z[3])
    spread(XC, xc, lambda o: f_mid, f_xc, fx_send, fx_recv, in_xc)
    f_xc[xc] = f_mid[...]
    collect(XC, xc, lambda o: f_mid, f_xc, fx_send, fx_recv)
    total = f_xc[0]
    for n in range(1, XC):
        total = total + f_xc[n]
    f_last[...] = total
    spread(TENSOR, t, lambda o: f_last, f_t, ft_send, ft_recv, in_t)
    f_t[t] = f_last[...]

    @pl.when(hop != 0)
    def _():
        lax.fori_loop(0, X, lambda quarter, carry: (right_z(quarter).wait_send(), carry)[1], 0)

    others(XC, xc, lambda o: right_x(o).wait_send())

    def sent_y(m, carry):
        to_plane(0, 1, y_send.at[0, m]).wait_send()
        to_plane(0, 1, y_send.at[1, m]).wait_send()
        to_plane(0, 1, y_again.at[m]).wait_send()
        return carry

    lax.fori_loop(0, 8, sent_y, 0)
    drain(TENSOR, t, lambda o: b_part.at[o], b_recv, b_send, b_rsem)
    drain(TENSOR, t, lambda o: b_sum, b_all, bg_send, bg_recv)
    drain(ZH, zh, lambda o: e_mine, e_z, ez_send, ez_recv)
    drain(XC, xc, lambda o: e_sum, e_xc, e_send, e_recv)
    drain(TENSOR, t, lambda o: e_mid, e_t, et_send, et_recv)
    drain(XC, xc, lambda o: a_part.at[o], a_xc, a_send, a_recv)
    drain(ZH, zh, lambda o: a_mid, a_z, az_send, az_recv)
    drain(XC, xc, lambda o: a_sum, a_all, ag_send, ag_recv)
    drain(ZH, zh, lambda o: f_part.at[o], f_z, fz_send, fz_recv)
    drain(XC, xc, lambda o: f_mid, f_xc, fx_send, fx_recv)
    others(ZH, zh, lambda o: left_z(o).wait_send())
    others(X, x, lambda o: left_x(o).wait_send())

    def sent_left_core(o, carry):
        left_core(o).wait_send()
        return carry

    lax.fori_loop(0, X, sent_left_core, 0)

    collect(TENSOR, t, lambda o: f_last, f_t, ft_send, ft_recv)
    total = f_t[0]
    for n in range(1, TENSOR):
        total = total + f_t[n]
    f_last_row = jnp.sum(
        jnp.where(lax.broadcasted_iota(jnp.int32, (8, 128), 0) == xc, total, 0.0), axis=0, keepdims=True
    )
    out_ref[...] = f_last_row[:, 0:Q]
    drain(TENSOR, t, lambda o: f_last, f_t, ft_send, ft_recv)


def on_device(
    query_acts, query_pos, query_feat, sae_enc, basis_in, basis_out, eigvals, train_in, train_out
):
    context = query_acts.shape[0]
    monitored = sae_enc.shape[0]
    vmem = pltpu.VMEM
    dma = pltpu.SemaphoreType.DMA
    scratch = [
        vmem((DIN // DP, context), bf16), vmem((monitored, DOUT // TENSOR), bf16),
        vmem((DIN // DP, I), bf16), vmem((J, DOUT // TENSOR), bf16), vmem((J, I), f32),
        vmem((R, DOUT), bf16),
        vmem((XC, R, JP), bf16), vmem((XC, R, JP), bf16), vmem((SEQS, R, JP), bf16), vmem((ZH, X, CORE, R, I), bf16),
        vmem((Q, J), f32), vmem((TENSOR, 8, JP), f32), vmem((TENSOR, 8, JP), f32), vmem((8, JP), f32),
        vmem((TENSOR, 8, JP), f32), vmem((Q, J), bf16),
        vmem((8, 128), f32), vmem((ZH, 8, 128), f32), vmem((8, 128), f32), vmem((XC, 8, 128), f32),
        vmem((8, 128), f32), vmem((TENSOR, 8, 128), f32),
        vmem((XC, 8, I), f32), vmem((XC, 8, I), f32), vmem((8, I), f32), vmem((ZH, 8, I), f32),
        vmem((8, I), f32), vmem((XC, 8, I), f32), vmem((Q, I), f32),
        vmem((2, J, I), bf16), vmem((2, Q, 128), f32), vmem((Q, 128), f32),
        vmem((ZH, 8, 128), f32), vmem((ZH, 8, 128), f32), vmem((8, 128), f32),
        vmem((XC, 8, 128), f32), vmem((8, 128), f32), vmem((TENSOR, 8, 128), f32),
        dma((7,)), dma((X,)), dma((X,)), dma((XC,)), dma((SEQS,)), dma((2, 8)), dma((8,)),
        dma((ZH,)), dma((ZH,)), dma((X,)), dma((X,)), dma((X,)), dma((X,)),
        dma((TENSOR,)), dma((TENSOR,)), dma((TENSOR,)), dma((TENSOR,)),
        dma((ZH,)), dma((ZH,)), dma((XC,)), dma((XC,)), dma((TENSOR,)), dma((TENSOR,)),
        dma((XC,)), dma((XC,)), dma((ZH,)), dma((ZH,)), dma((XC,)), dma((XC,)),
        dma((ZH,)), dma((ZH,)), dma((XC,)), dma((XC,)), dma((TENSOR,)), dma((TENSOR,)),
    ]
    anywhere = pl.BlockSpec(memory_space=pl.ANY)
    inside = pl.BlockSpec(memory_space=pltpu.VMEM)
    return pl.pallas_call(
        kernel,
        out_shape=jax.ShapeDtypeStruct((1, Q), f32),
        in_specs=[inside, inside] + [anywhere] * 7,
        out_specs=inside,
        scratch_shapes=scratch,
        compiler_params=pltpu.CompilerParams(
            collective_id=0, has_side_effects=True, vmem_limit_bytes=56 << 20
        ),
        name="influence",
    )(
        query_pos.reshape(1, Q), query_feat.reshape(1, Q), query_acts.T, sae_enc, basis_in, basis_out.T,
        eigvals.T, train_in.reshape(R, I), train_out.reshape(R, DOUT),
    ).reshape(Q, 1)


def solution(mesh):
    in_specs = (
        P(None, "dp"),
        P(),
        P(),
        P(None, "tensor"),
        P("dp", "tensor"),
        P("tensor", "dp"),
        P("tensor", "dp"),
        P("dp", None, "tensor"),
        P("dp", None, None),
    )
    out_specs = P(None, "dp")
    return jax.shard_map(
        on_device, mesh=mesh, in_specs=in_specs, out_specs=out_specs, check_vma=False
    )
```

```python
import math

import jax
import jax.numpy as jnp
from jax import lax
from jax.experimental import pallas as pl
from jax.experimental.pallas import tpu as pltpu
from jax.sharding import PartitionSpec as P

DIN = 5120
DOUT = 27648
R = 32
damping = 0.1

ZH, X, CORE, Y, ZL = 4, 4, 2, 4, 2
XC = X * CORE
DP = ZH * XC
TENSOR = Y * ZL
SEQS = 32
Q = 64
I = DIN // TENSOR
J = DOUT // DP
JP = 896
MESH = pl.DeviceIdType.MESH
f32 = jnp.float32
bf16 = jnp.bfloat16
FIRST_ROWS = (((0,), (0,)), ((), ()))
LAST_COLUMNS = (((1,), (1,)), ((), ()))


def wrap(v, n):
    return jnp.where(v >= n, v - n, v)


def half_of(v):
    return jnp.where(v >= 4, jnp.where(v >= 6, 3, 2), jnp.where(v >= 2, 1, 0))


def kernel(
    pos_ref, feat_ref, acts_hbm, sae_hbm, bin_hbm, bout_hbm, eig_hbm, tin_hbm, tout_hbm,
    out_ref,
    acts, sae, bin_, bout, inv, tout, right_out, right_row, right, left,
    b_mine, b_part, b_recv, b_sum, b_all, b_lo,
    e_mine, e_z, e_sum, e_xc, e_mid, e_t,
    a_part, a_xc, a_mid, a_z, a_sum, a_all, a_full,
    damped, rows, scores, f_part, f_z, f_mid, f_xc, f_last, f_t,
    local_sem, rz_send, rz_recv, r_send, r_recv, y_send, y_again, lz_send, lz_recv, lx_send, lx_recv, lc_send, lc_recv,
    b_send, b_rsem, bg_send, bg_recv, ez_send, ez_recv, e_send, e_recv, et_send, et_recv,
    a_send, a_recv, az_send, az_recv, ag_send, ag_recv,
    fz_send, fz_recv, fx_send, fx_recv, ft_send, ft_recv,
):
    d = lax.axis_index("dp")
    t = lax.axis_index("tensor")
    zh, xc = lax.div(d, XC), lax.rem(d, XC)
    x, core = lax.div(xc, CORE), lax.rem(xc, CORE)
    y, zl = lax.div(t, ZL), lax.rem(t, ZL)

    def remote(src, dst, send, recv, dp, tensor):
        return pltpu.make_async_remote_copy(
            src_ref=src, dst_ref=dst, send_sem=send, recv_sem=recv,
            device_id={"dp": dp, "tensor": tensor}, device_id_type=MESH,
        )

    def total_of(ref, count):
        total = ref[0]
        for n in range(1, count):
            total = total + ref[n]
        return total

    def others(count, me, body):
        def step(k, carry):
            body(wrap(me + k, count))
            return carry

        lax.fori_loop(1, count, step, 0)

    def spread(count, me, src, dst, send, recv, place):
        def body(o):
            dp, tensor = place(o)
            remote(src(o), dst.at[me], send.at[o], recv.at[me], dp, tensor).start()

        others(count, me, body)

    def collect(count, me, src, dst, send, recv):
        def body(o):
            remote(src(o), dst.at[o], send.at[o], recv.at[o], d, t).wait_recv()

        others(count, me, body)

    def drain(count, me, src, dst, send, recv):
        def body(o):
            remote(src(o), dst.at[me], send.at[o], recv.at[me], d, t).wait_send()

        others(count, me, body)

    in_xc = lambda o: (zh * XC + o, t)
    in_zh = lambda o: (o * XC + xc, t)
    in_t = lambda o: (d, o)

    loads = [
        pltpu.make_async_copy(src, dst, local_sem.at[n])
        for n, (src, dst) in enumerate((
            (tout_hbm, tout), (tin_hbm, left.at[zh, x, core]), (eig_hbm, inv), (acts_hbm, acts), (bin_hbm, bin_),
            (sae_hbm, sae), (bout_hbm, bout),
        ))
    ]
    for load in loads:
        load.start()
    l_tout, l_tin, l_eig, l_acts, l_bin, l_sae, l_bout = loads

    barrier = pltpu.get_barrier_semaphore()

    def greet(place):
        def body(o):
            dp, tensor = place(o)
            pl.semaphore_signal(barrier, inc=1, device_id={"dp": dp, "tensor": tensor}, device_id_type=MESH)

        return body

    others(ZH, zh, greet(in_zh))
    others(TENSOR, t, greet(in_t))
    others(XC, xc, greet(in_xc))

    def low_two(v):
        return wrap(wrap(v, 8), 4)

    odd_zh = zh - 2 * half_of(zh)

    def hop_of(sx, sc, plane):
        off = low_two(sx + jnp.where(sc == zl, 0, 1) + 2 * zl - plane + Y)
        flip = jnp.logical_and(odd_zh == 1, jnp.logical_or(off == 0, off == 2))
        return wrap(off + jnp.where(flip, 2, 0), ZH)

    hop = hop_of(x, core, y)
    row = wrap(zh + hop, ZH)
    column_seq = wrap(zh - hop + ZH, ZH) * XC + xc

    l_tout.wait()

    def four(half, carry):
        wide = tout[:, pl.ds(pl.multiple_of((2 * row + half) * (4 * J), 128), 4 * J)]
        for p in range(4):
            right_out[half * 4 + p, :, 0:J] = wide[:, p * J:(p + 1) * J]
        return carry

    lax.fori_loop(0, 2, four, 0)

    l_eig.wait()

    def fold(n, total):
        some = inv[pl.ds(pl.multiple_of(n * 96, 8), 96), :]
        some = jnp.sum(some.reshape(12, 8, I), axis=0)
        for c in range(I // 128):
            total = total + some[:, c * 128:(c + 1) * 128]
        return total

    e_part = lax.fori_loop(0, J // 96, fold, jnp.zeros((8, 128), f32))
    e_mine[...] = e_part
    e_z[zh] = e_part
    l_tin.wait()

    pl.semaphore_wait(barrier, ZH + TENSOR + XC - 3)
    spread(ZH, zh, lambda o: e_mine, e_z, ez_send, ez_recv, in_zh)

    def left_z(o):
        return remote(left.at[zh, x, core], left.at[zh, x, core], lz_send.at[o], lz_recv.at[zh],
                      o * XC + xc, t)

    others(ZH, zh, lambda o: left_z(o).start())

    def right_z(quarter):
        blocks = pl.ds(wrap(x + quarter, X) * CORE, CORE)
        return remote(right_out.at[blocks], right_row.at[blocks], rz_send.at[quarter], rz_recv.at[quarter],
                      row * XC + xc, t)

    def right_z_start(first, last):
        @pl.when(hop != 0)
        def _():
            lax.fori_loop(first, last, lambda quarter, carry: (right_z(quarter).start(), carry)[1], 0)

        @pl.when(hop == 0)
        def _():
            def here(quarter, carry):
                blocks = pl.ds(wrap(x + quarter, X) * CORE, CORE)
                pltpu.make_async_copy(right_out.at[blocks], right_row.at[blocks], rz_recv.at[quarter]).start()
                return carry

            lax.fori_loop(first, last, here, 0)

    right_z_start(0, 2)

    l_sae.wait()
    monitored = sae.shape[0]
    chooser = jnp.where(
        lax.broadcasted_iota(jnp.int32, (monitored, Q), 0) == feat_ref[...], 1.0, 0.0
    ).astype(bf16)
    l_bout.wait()
    wide = 384
    b_mine[...] = jnp.zeros_like(b_mine)

    def b_step(n, carry):
        columns = pl.ds(pl.multiple_of(n * wide, 128), wide)
        outputs = lax.dot_general(
            chooser, sae[:, columns], FIRST_ROWS, preferred_element_type=f32
        ).astype(bf16)
        b_mine[...] += lax.dot_general(
            outputs, bout[:, columns], LAST_COLUMNS, preferred_element_type=f32
        )
        return carry

    lax.fori_loop(0, DOUT // TENSOR // wide, b_step, 0)
    for n in range(TENSOR):
        b_part[n, :, 0:J] = b_mine[8 * n:8 * (n + 1), :]
    spread(TENSOR, t, lambda o: b_part.at[o], b_recv, b_send, b_rsem, in_t)
    b_recv[t] = b_part[t]

    l_acts.wait()
    context = acts.shape[1]
    picker = jnp.where(
        lax.broadcasted_iota(jnp.int32, (context, Q), 0) == pos_ref[...], 1.0, 0.0
    ).astype(bf16)
    inputs = jnp.dot(acts[...], picker, preferred_element_type=f32).astype(bf16)
    l_bin.wait()
    a_mine = lax.dot_general(inputs, bin_[...], FIRST_ROWS, preferred_element_type=f32)
    for n in range(XC):
        a_part[n] = a_mine[8 * n:8 * (n + 1)]
    spread(XC, xc, lambda o: a_part.at[o], a_xc, a_send, a_recv, in_xc)
    a_xc[xc] = a_part[xc]

    right_z_start(2, X)

    collect(ZH, zh, lambda o: e_mine, e_z, ez_send, ez_recv)
    e_sum[...] = total_of(e_z, ZH)
    spread(XC, xc, lambda o: e_sum, e_xc, e_send, e_recv, in_xc)
    e_xc[xc] = e_sum[...]

    def left_x(o):
        return remote(left.at[:, x, core], left.at[:, x, core], lx_send.at[o], lx_recv.at[x],
                      zh * XC + o * CORE + core, t)

    def left_core(o):
        return remote(left.at[:, o, core], left.at[:, o, core], lc_send.at[o], lc_recv.at[o],
                      zh * XC + x * CORE + (1 - core), t)

    others(ZH, zh, lambda o: remote(
        left.at[o, x, core], left.at[o, x, core], lz_send.at[o], lz_recv.at[o], d, t).wait_recv())
    others(X, x, lambda o: left_x(o).start())
    left_core(x).start()

    def right_x(o):
        return remote(right_row.at[o], right.at[column_seq], r_send.at[o], r_recv.at[column_seq],
                      zh * XC + o, t)

    def right_quarter(quarter):
        right_z(quarter).wait_recv()

        def one(c, carry):
            o = wrap(x + quarter, X) * CORE + c

            @pl.when(o != xc)
            def _():
                right_x(o).start()

            @pl.when(o == xc)
            def _():
                pltpu.make_async_copy(right_row.at[o], right.at[column_seq], r_recv.at[column_seq]).start()

            return carry

        lax.fori_loop(0, CORE, one, 0)

    def seq_of(k):
        g = jnp.where(k >= 16, jnp.where(k >= 24, 3, 2), jnp.where(k >= 8, 1, 0))
        m = k - 8 * g
        off = jnp.where(g == 0, 0, jnp.where(g == 3, 2, jnp.where((g == 1) == (m < 4), 1, 3)))
        pair = half_of(m)
        sx, sc = wrap(x - pair + X, X), m - 2 * pair
        return wrap(zh - hop_of(sx, sc, wrap(y + off, Y)) + ZH, ZH), sx, sc

    def flat(s):
        return (s[0] * X + s[1]) * CORE + s[2]

    def right_wait(s):
        remote(right.at[s], right.at[s], y_again.at[0], r_recv.at[s], d, t).wait_recv()

    def to_plane(s, off, sem):
        return remote(right.at[s], right.at[s], sem, r_recv.at[s], d, wrap(y + off, Y) * ZL + zl)

    def own(m, carry):
        s = flat(seq_of(m))
        right_wait(s)
        to_plane(s, 1, y_send.at[0, m]).start()
        to_plane(s, 3, y_send.at[1, m]).start()
        return carry

    right_quarter(0)
    right_quarter(1)

    collect(XC, xc, lambda o: a_part.at[o], a_xc, a_send, a_recv)
    a_mid[...] = total_of(a_xc, XC)
    spread(ZH, zh, lambda o: a_mid, a_z, az_send, az_recv, in_zh)
    a_z[zh] = a_mid[...]

    collect(TENSOR, t, lambda o: b_part.at[o], b_recv, b_send, b_rsem)
    b_sum[...] = total_of(b_recv, TENSOR)
    spread(TENSOR, t, lambda o: b_sum, b_all, bg_send, bg_recv, in_t)
    b_all[t] = b_sum[...]

    collect(XC, xc, lambda o: e_sum, e_xc, e_send, e_recv)
    e_mid[...] = total_of(e_xc, XC)
    spread(TENSOR, t, lambda o: e_mid, e_t, et_send, et_recv, in_t)
    e_t[t] = e_mid[...]

    lax.fori_loop(0, 2, own, 0)
    right_quarter(2)
    lax.fori_loop(2, 4, own, 0)
    right_quarter(3)

    collect(ZH, zh, lambda o: a_mid, a_z, az_send, az_recv)
    a_sum[...] = total_of(a_z, ZH) * (1.0 / math.sqrt(DIN * DOUT * R))
    spread(XC, xc, lambda o: a_sum, a_all, ag_send, ag_recv, in_xc)
    a_all[xc] = a_sum[...]

    def left_x_wait(o):
        remote(left.at[:, o, core], left.at[:, o, core], lx_send.at[o], lx_recv.at[o], d, t).wait_recv()
        left_core(o).start()

    others(X, x, left_x_wait)
    lax.fori_loop(4, 6, own, 0)

    collect(TENSOR, t, lambda o: e_mid, e_t, et_send, et_recv)
    shift = damping * (jnp.sum(total_of(e_t, TENSOR)) / (DIN * DOUT))

    def invert(n, carry):
        some = pl.ds(pl.multiple_of(n * 96, 8), 96)
        inv[some, :] = 1.0 / (inv[some, :] + shift)
        return carry

    lax.fori_loop(0, J // 96, invert, 0)

    collect(TENSOR, t, lambda o: b_sum, b_all, bg_send, bg_recv)
    for n in range(TENSOR // 2):
        pair = jnp.concatenate([b_all[2 * n], b_all[2 * n + 1]], axis=0)
        b_lo[16 * n:16 * (n + 1), :] = pair.astype(bf16)[:, 0:J]

    lax.fori_loop(6, 8, own, 0)

    def left_core_wait(o, carry):
        remote(left.at[:, o, 1 - core], left.at[:, o, 1 - core], lc_send.at[o], lc_recv.at[o], d, t).wait_recv()
        return carry

    lax.fori_loop(0, X, left_core_wait, 0)

    collect(XC, xc, lambda o: a_sum, a_all, ag_send, ag_recv)
    for n in range(XC):
        a_full[8 * n:8 * (n + 1), :] = a_all[n]

    def ready(part):
        def arrived(k, carry):
            right_wait(flat(seq_of(k)))
            return carry

        def arrived_and_on(k, carry):
            s = flat(seq_of(k))
            right_wait(s)
            m = k - 8
            to_plane(s, jnp.where(m < 4, 3, 1), y_again.at[m]).start()
            return carry

        first = part * 4

        @pl.when(jnp.logical_and(part >= 2, part < 4))
        def _():
            lax.fori_loop(first, first + 4, arrived_and_on, 0)

        @pl.when(part >= 4)
        def _():
            lax.fori_loop(first, first + 4, arrived, 0)

    def cross(s, slot):
        wide = lax.dot_general(
            right[flat(s), :, 0:J], left[s[0], s[1], s[2]], FIRST_ROWS, preferred_element_type=f32
        )
        damped[slot] = (wide * inv[...]).astype(bf16)

    def project(slot):
        part = jnp.dot(b_lo[...], damped[slot], preferred_element_type=f32) * a_full[...]
        row = part[:, 0:128]
        for n in range(1, I // 128):
            row = row + part[:, n * 128:(n + 1) * 128]
        rows[slot] = row

    def score(of, slot):
        row = jnp.sum(rows[slot], axis=1, keepdims=True)
        lane = lax.broadcasted_iota(jnp.int32, (Q, 128), 1)
        scores[...] = jnp.where(lane == of, row, scores[...])

    def step(k, before, slot):
        s = seq_of(k)
        cross(s, slot)
        project(1 - slot)
        score(before[0], slot)
        return before[1], flat(s)

    scores[...] = jnp.zeros_like(scores)
    rows[...] = jnp.zeros_like(rows)
    damped[1] = jnp.zeros((J, I), bf16)

    def eighth(part, before):
        ready(part)

        def two(h, before):
            before = step(part * 4 + 2 * h, before, 0)
            return step(part * 4 + 2 * h + 1, before, 1)

        return lax.fori_loop(0, 2, two, before)

    before = lax.fori_loop(0, SEQS // 4, eighth, (-1, -1))
    project(1)
    score(before[0], 0)
    score(before[1], 1)

    by_seq = scores[...].T
    for n in range(ZH):
        f_part[n, :, 0:Q] = by_seq[8 * n:8 * (n + 1), :]
        f_part[n, :, Q:128] = jnp.zeros((8, 128 - Q), f32)
    spread(ZH, zh, lambda o: f_part.at[o], f_z, fz_send, fz_recv, in_zh)
    f_z[zh] = f_part[zh]
    collect(ZH, zh, lambda o: f_part.at[o], f_z, fz_send, fz_recv)
    f_mid[...] = (f_z[0] + f_z[1]) + (f_z[2] + f_z[3])
    spread(XC, xc, lambda o: f_mid, f_xc, fx_send, fx_recv, in_xc)
    f_xc[xc] = f_mid[...]
    collect(XC, xc, lambda o: f_mid, f_xc, fx_send, fx_recv)
    total = f_xc[0]
    for n in range(1, XC):
        total = total + f_xc[n]
    f_last[...] = total
    spread(TENSOR, t, lambda o: f_last, f_t, ft_send, ft_recv, in_t)
    f_t[t] = f_last[...]

    @pl.when(hop != 0)
    def _():
        lax.fori_loop(0, X, lambda quarter, carry: (right_z(quarter).wait_send(), carry)[1], 0)

    others(XC, xc, lambda o: right_x(o).wait_send())

    def sent_y(m, carry):
        to_plane(0, 1, y_send.at[0, m]).wait_send()
        to_plane(0, 1, y_send.at[1, m]).wait_send()
        to_plane(0, 1, y_again.at[m]).wait_send()
        return carry

    lax.fori_loop(0, 8, sent_y, 0)
    drain(TENSOR, t, lambda o: b_part.at[o], b_recv, b_send, b_rsem)
    drain(TENSOR, t, lambda o: b_sum, b_all, bg_send, bg_recv)
    drain(ZH, zh, lambda o: e_mine, e_z, ez_send, ez_recv)
    drain(XC, xc, lambda o: e_sum, e_xc, e_send, e_recv)
    drain(TENSOR, t, lambda o: e_mid, e_t, et_send, et_recv)
    drain(XC, xc, lambda o: a_part.at[o], a_xc, a_send, a_recv)
    drain(ZH, zh, lambda o: a_mid, a_z, az_send, az_recv)
    drain(XC, xc, lambda o: a_sum, a_all, ag_send, ag_recv)
    drain(ZH, zh, lambda o: f_part.at[o], f_z, fz_send, fz_recv)
    drain(XC, xc, lambda o: f_mid, f_xc, fx_send, fx_recv)
    others(ZH, zh, lambda o: left_z(o).wait_send())
    others(X, x, lambda o: left_x(o).wait_send())

    def sent_left_core(o, carry):
        left_core(o).wait_send()
        return carry

    lax.fori_loop(0, X, sent_left_core, 0)

    collect(TENSOR, t, lambda o: f_last, f_t, ft_send, ft_recv)
    total = f_t[0]
    for n in range(1, TENSOR):
        total = total + f_t[n]
    f_last_row = jnp.sum(
        jnp.where(lax.broadcasted_iota(jnp.int32, (8, 128), 0) == xc, total, 0.0), axis=0, keepdims=True
    )
    out_ref[...] = f_last_row[:, 0:Q]
    drain(TENSOR, t, lambda o: f_last, f_t, ft_send, ft_recv)


def on_device(
    query_acts, query_pos, query_feat, sae_enc, basis_in, basis_out, eigvals, train_in, train_out
):
    context = query_acts.shape[0]
    monitored = sae_enc.shape[0]
    vmem = pltpu.VMEM
    dma = pltpu.SemaphoreType.DMA
    scratch = [
        vmem((DIN // DP, context), bf16), vmem((monitored, DOUT // TENSOR), bf16),
        vmem((DIN // DP, I), bf16), vmem((J, DOUT // TENSOR), bf16), vmem((J, I), f32),
        vmem((R, DOUT), bf16),
        vmem((XC, R, JP), bf16), vmem((XC, R, JP), bf16), vmem((SEQS, R, JP), bf16), vmem((ZH, X, CORE, R, I), bf16),
        vmem((Q, J), f32), vmem((TENSOR, 8, JP), f32), vmem((TENSOR, 8, JP), f32), vmem((8, JP), f32),
        vmem((TENSOR, 8, JP), f32), vmem((Q, J), bf16),
        vmem((8, 128), f32), vmem((ZH, 8, 128), f32), vmem((8, 128), f32), vmem((XC, 8, 128), f32),
        vmem((8, 128), f32), vmem((TENSOR, 8, 128), f32),
        vmem((XC, 8, I), f32), vmem((XC, 8, I), f32), vmem((8, I), f32), vmem((ZH, 8, I), f32),
        vmem((8, I), f32), vmem((XC, 8, I), f32), vmem((Q, I), f32),
        vmem((2, J, I), bf16), vmem((2, Q, 128), f32), vmem((Q, 128), f32),
        vmem((ZH, 8, 128), f32), vmem((ZH, 8, 128), f32), vmem((8, 128), f32),
        vmem((XC, 8, 128), f32), vmem((8, 128), f32), vmem((TENSOR, 8, 128), f32),
        dma((7,)), dma((X,)), dma((X,)), dma((XC,)), dma((SEQS,)), dma((2, 8)), dma((8,)),
        dma((ZH,)), dma((ZH,)), dma((X,)), dma((X,)), dma((X,)), dma((X,)),
        dma((TENSOR,)), dma((TENSOR,)), dma((TENSOR,)), dma((TENSOR,)),
        dma((ZH,)), dma((ZH,)), dma((XC,)), dma((XC,)), dma((TENSOR,)), dma((TENSOR,)),
        dma((XC,)), dma((XC,)), dma((ZH,)), dma((ZH,)), dma((XC,)), dma((XC,)),
        dma((ZH,)), dma((ZH,)), dma((XC,)), dma((XC,)), dma((TENSOR,)), dma((TENSOR,)),
    ]
    anywhere = pl.BlockSpec(memory_space=pl.ANY)
    inside = pl.BlockSpec(memory_space=pltpu.VMEM)
    return pl.pallas_call(
        kernel,
        out_shape=jax.ShapeDtypeStruct((1, Q), f32),
        in_specs=[inside, inside] + [anywhere] * 7,
        out_specs=inside,
        scratch_shapes=scratch,
        compiler_params=pltpu.CompilerParams(
            collective_id=0, has_side_effects=True, vmem_limit_bytes=56 << 20
        ),
        name="influence",
    )(
        query_pos.reshape(1, Q), query_feat.reshape(1, Q), query_acts.T, sae_enc, basis_in, basis_out.T,
        eigvals.T, train_in.reshape(R, I), train_out.reshape(R, DOUT),
    ).reshape(Q, 1)


def solution(mesh):
    in_specs = (
        P(None, "dp"),
        P(),
        P(),
        P(None, "tensor"),
        P("dp", "tensor"),
        P("tensor", "dp"),
        P("tensor", "dp"),
        P("dp", None, "tensor"),
        P("dp", None, None),
    )
    out_specs = P(None, "dp")
    return jax.shard_map(
        on_device, mesh=mesh, in_specs=in_specs, out_specs=out_specs, check_vma=False
    )
```

```python
import math

import jax
import jax.numpy as jnp
from jax import lax
from jax.experimental import pallas as pl
from jax.experimental.pallas import tpu as pltpu
from jax.sharding import PartitionSpec as P

DIN = 5120
DOUT = 27648
R = 32
damping = 0.1

ZH, X, CORE, Y, ZL = 4, 4, 2, 4, 2
XC = X * CORE
DP = ZH * XC
TENSOR = Y * ZL
SEQS = 32
Q = 64
I = DIN // TENSOR
J = DOUT // DP
JP = 896
MESH = pl.DeviceIdType.MESH
f32 = jnp.float32
bf16 = jnp.bfloat16
FIRST_ROWS = (((0,), (0,)), ((), ()))
LAST_COLUMNS = (((1,), (1,)), ((), ()))


def wrap(v, n):
    return jnp.where(v >= n, v - n, v)


def half_of(v):
    return jnp.where(v >= 4, jnp.where(v >= 6, 3, 2), jnp.where(v >= 2, 1, 0))


def kernel(
    pos_ref, feat_ref, acts_hbm, sae_hbm, bin_hbm, bout_hbm, eig_hbm, tin_hbm, tout_hbm,
    out_ref,
    acts, sae, bin_, bout, inv, tout, right_out, right_row, right, left,
    b_mine, b_part, b_recv, b_sum, b_all, b_lo,
    e_mine, e_z, e_sum, e_xc, e_mid, e_t,
    a_part, a_xc, a_mid, a_z, a_sum, a_all, a_full,
    damped, rows, scores, f_part, f_z, f_mid, f_xc, f_last, f_t,
    local_sem, rz_send, rz_recv, r_send, r_recv, y_send, y_again, lz_send, lz_recv, lx_send, lx_recv, lc_send, lc_recv,
    b_send, b_rsem, bg_send, bg_recv, ez_send, ez_recv, e_send, e_recv, et_send, et_recv,
    a_send, a_recv, az_send, az_recv, ag_send, ag_recv,
    fz_send, fz_recv, fx_send, fx_recv, ft_send, ft_recv,
):
    d = lax.axis_index("dp")
    t = lax.axis_index("tensor")
    zh, xc = lax.div(d, XC), lax.rem(d, XC)
    x, core = lax.div(xc, CORE), lax.rem(xc, CORE)
    y, zl = lax.div(t, ZL), lax.rem(t, ZL)

    def remote(src, dst, send, recv, dp, tensor):
        return pltpu.make_async_remote_copy(
            src_ref=src, dst_ref=dst, send_sem=send, recv_sem=recv,
            device_id={"dp": dp, "tensor": tensor}, device_id_type=MESH,
        )

    def total_of(ref, count):
        total = ref[0]
        for n in range(1, count):
            total = total + ref[n]
        return total

    def others(count, me, body):
        def step(k, carry):
            body(wrap(me + k, count))
            return carry

        lax.fori_loop(1, count, step, 0)

    def spread(count, me, src, dst, send, recv, place):
        def body(o):
            dp, tensor = place(o)
            remote(src(o), dst.at[me], send.at[o], recv.at[me], dp, tensor).start()

        others(count, me, body)

    def collect(count, me, src, dst, send, recv):
        def body(o):
            remote(src(o), dst.at[o], send.at[o], recv.at[o], d, t).wait_recv()

        others(count, me, body)

    def drain(count, me, src, dst, send, recv):
        def body(o):
            remote(src(o), dst.at[me], send.at[o], recv.at[me], d, t).wait_send()

        others(count, me, body)

    in_xc = lambda o: (zh * XC + o, t)
    in_zh = lambda o: (o * XC + xc, t)
    in_t = lambda o: (d, o)

    loads = [
        pltpu.make_async_copy(src, dst, local_sem.at[n])
        for n, (src, dst) in enumerate((
            (tout_hbm, tout), (tin_hbm, left.at[zh, x, core]), (eig_hbm, inv), (acts_hbm, acts), (bin_hbm, bin_),
            (sae_hbm, sae), (bout_hbm, bout),
        ))
    ]
    for load in loads:
        load.start()
    l_tout, l_tin, l_eig, l_acts, l_bin, l_sae, l_bout = loads

    barrier = pltpu.get_barrier_semaphore()

    def greet(place):
        def body(o):
            dp, tensor = place(o)
            pl.semaphore_signal(barrier, inc=1, device_id={"dp": dp, "tensor": tensor}, device_id_type=MESH)

        return body

    others(ZH, zh, greet(in_zh))
    others(TENSOR, t, greet(in_t))
    others(XC, xc, greet(in_xc))

    def low_two(v):
        return wrap(wrap(v, 8), 4)

    odd_zh = zh - 2 * half_of(zh)

    def hop_of(sx, sc, plane):
        off = low_two(sx + jnp.where(sc == zl, 0, 1) + 2 * zl - plane + Y)
        flip = jnp.logical_and(odd_zh == 1, jnp.logical_or(off == 0, off == 2))
        return wrap(off + jnp.where(flip, 2, 0), ZH)

    hop = hop_of(x, core, y)
    row = wrap(zh + hop, ZH)
    column_seq = wrap(zh - hop + ZH, ZH) * XC + xc

    l_tout.wait()

    def four(half, carry):
        wide = tout[:, pl.ds(pl.multiple_of((2 * row + half) * (4 * J), 128), 4 * J)]
        for p in range(4):
            right_out[half * 4 + p, :, 0:J] = wide[:, p * J:(p + 1) * J]
        return carry

    lax.fori_loop(0, 2, four, 0)

    l_eig.wait()

    def fold(n, total):
        some = inv[pl.ds(pl.multiple_of(n * 96, 8), 96), :]
        some = jnp.sum(some.reshape(12, 8, I), axis=0)
        for c in range(I // 128):
            total = total + some[:, c * 128:(c + 1) * 128]
        return total

    e_part = lax.fori_loop(0, J // 96, fold, jnp.zeros((8, 128), f32))
    e_mine[...] = e_part
    e_z[zh] = e_part
    l_tin.wait()

    pl.semaphore_wait(barrier, ZH + TENSOR + XC - 3)
    spread(ZH, zh, lambda o: e_mine, e_z, ez_send, ez_recv, in_zh)

    def left_z(o):
        return remote(left.at[zh, x, core], left.at[zh, x, core], lz_send.at[o], lz_recv.at[zh],
                      o * XC + xc, t)

    others(ZH, zh, lambda o: left_z(o).start())

    def right_z(quarter):
        blocks = pl.ds(wrap(x + quarter, X) * CORE, CORE)
        return remote(right_out.at[blocks], right_row.at[blocks], rz_send.at[quarter], rz_recv.at[quarter],
                      row * XC + xc, t)

    def right_z_start(first, last):
        @pl.when(hop != 0)
        def _():
            lax.fori_loop(first, last, lambda quarter, carry: (right_z(quarter).start(), carry)[1], 0)

        @pl.when(hop == 0)
        def _():
            def here(quarter, carry):
                blocks = pl.ds(wrap(x + quarter, X) * CORE, CORE)
                pltpu.make_async_copy(right_out.at[blocks], right_row.at[blocks], rz_recv.at[quarter]).start()
                return carry

            lax.fori_loop(first, last, here, 0)

    right_z_start(0, 2)

    l_sae.wait()
    monitored = sae.shape[0]
    chooser = jnp.where(
        lax.broadcasted_iota(jnp.int32, (monitored, Q), 0) == feat_ref[...], 1.0, 0.0
    ).astype(bf16)
    l_bout.wait()
    wide = 384
    b_mine[...] = jnp.zeros_like(b_mine)

    def b_step(n, carry):
        columns = pl.ds(pl.multiple_of(n * wide, 128), wide)
        outputs = lax.dot_general(
            chooser, sae[:, columns], FIRST_ROWS, preferred_element_type=f32
        ).astype(bf16)
        b_mine[...] += lax.dot_general(
            outputs, bout[:, columns], LAST_COLUMNS, preferred_element_type=f32
        )
        return carry

    lax.fori_loop(0, DOUT // TENSOR // wide, b_step, 0)
    for n in range(TENSOR):
        b_part[n, :, 0:J] = b_mine[8 * n:8 * (n + 1), :]
    spread(TENSOR, t, lambda o: b_part.at[o], b_recv, b_send, b_rsem, in_t)
    b_recv[t] = b_part[t]

    l_acts.wait()
    context = acts.shape[1]
    picker = jnp.where(
        lax.broadcasted_iota(jnp.int32, (context, Q), 0) == pos_ref[...], 1.0, 0.0
    ).astype(bf16)
    inputs = jnp.dot(acts[...], picker, preferred_element_type=f32).astype(bf16)
    l_bin.wait()
    a_mine = lax.dot_general(inputs, bin_[...], FIRST_ROWS, preferred_element_type=f32)
    for n in range(XC):
        a_part[n] = a_mine[8 * n:8 * (n + 1)]
    spread(XC, xc, lambda o: a_part.at[o], a_xc, a_send, a_recv, in_xc)
    a_xc[xc] = a_part[xc]

    right_z_start(2, X)

    collect(ZH, zh, lambda o: e_mine, e_z, ez_send, ez_recv)
    e_sum[...] = total_of(e_z, ZH)
    spread(XC, xc, lambda o: e_sum, e_xc, e_send, e_recv, in_xc)
    e_xc[xc] = e_sum[...]

    def left_x(o):
        return remote(left.at[:, x, core], left.at[:, x, core], lx_send.at[o], lx_recv.at[x],
                      zh * XC + o * CORE + core, t)

    def left_core(o):
        return remote(left.at[:, o, core], left.at[:, o, core], lc_send.at[o], lc_recv.at[o],
                      zh * XC + x * CORE + (1 - core), t)

    others(ZH, zh, lambda o: remote(
        left.at[o, x, core], left.at[o, x, core], lz_send.at[o], lz_recv.at[o], d, t).wait_recv())
    others(X, x, lambda o: left_x(o).start())
    left_core(x).start()

    def right_x(o):
        return remote(right_row.at[o], right.at[column_seq], r_send.at[o], r_recv.at[column_seq],
                      zh * XC + o, t)

    def right_quarter(quarter):
        right_z(quarter).wait_recv()

        def one(c, carry):
            o = wrap(x + quarter, X) * CORE + c

            @pl.when(o != xc)
            def _():
                right_x(o).start()

            @pl.when(o == xc)
            def _():
                pltpu.make_async_copy(right_row.at[o], right.at[column_seq], r_recv.at[column_seq]).start()

            return carry

        lax.fori_loop(0, CORE, one, 0)

    def seq_of(k):
        g = jnp.where(k >= 16, jnp.where(k >= 24, 3, 2), jnp.where(k >= 8, 1, 0))
        m = k - 8 * g
        off = jnp.where(g == 0, 0, jnp.where(g == 3, 2, jnp.where((g == 1) == (m < 4), 1, 3)))
        pair = half_of(m)
        sx, sc = wrap(x - pair + X, X), m - 2 * pair
        return wrap(zh - hop_of(sx, sc, wrap(y + off, Y)) + ZH, ZH), sx, sc

    def flat(s):
        return (s[0] * X + s[1]) * CORE + s[2]

    def right_wait(s):
        remote(right.at[s], right.at[s], y_again.at[0], r_recv.at[s], d, t).wait_recv()

    def to_plane(s, off, sem):
        return remote(right.at[s], right.at[s], sem, r_recv.at[s], d, wrap(y + off, Y) * ZL + zl)

    def own(m, carry):
        s = flat(seq_of(m))
        right_wait(s)
        to_plane(s, 1, y_send.at[0, m]).start()
        to_plane(s, 3, y_send.at[1, m]).start()
        return carry

    right_quarter(0)
    right_quarter(1)

    collect(XC, xc, lambda o: a_part.at[o], a_xc, a_send, a_recv)
    a_mid[...] = total_of(a_xc, XC)
    spread(ZH, zh, lambda o: a_mid, a_z, az_send, az_recv, in_zh)
    a_z[zh] = a_mid[...]

    collect(TENSOR, t, lambda o: b_part.at[o], b_recv, b_send, b_rsem)
    b_sum[...] = total_of(b_recv, TENSOR)
    spread(TENSOR, t, lambda o: b_sum, b_all, bg_send, bg_recv, in_t)
    b_all[t] = b_sum[...]

    collect(XC, xc, lambda o: e_sum, e_xc, e_send, e_recv)
    e_mid[...] = total_of(e_xc, XC)
    spread(TENSOR, t, lambda o: e_mid, e_t, et_send, et_recv, in_t)
    e_t[t] = e_mid[...]

    lax.fori_loop(0, 2, own, 0)
    right_quarter(2)
    lax.fori_loop(2, 4, own, 0)
    right_quarter(3)

    collect(ZH, zh, lambda o: a_mid, a_z, az_send, az_recv)
    a_sum[...] = total_of(a_z, ZH) * (1.0 / math.sqrt(DIN * DOUT * R))
    spread(XC, xc, lambda o: a_sum, a_all, ag_send, ag_recv, in_xc)
    a_all[xc] = a_sum[...]

    def left_x_wait(o):
        remote(left.at[:, o, core], left.at[:, o, core], lx_send.at[o], lx_recv.at[o], d, t).wait_recv()
        left_core(o).start()

    others(X, x, left_x_wait)
    lax.fori_loop(4, 6, own, 0)

    collect(TENSOR, t, lambda o: e_mid, e_t, et_send, et_recv)
    shift = damping * (jnp.sum(total_of(e_t, TENSOR)) / (DIN * DOUT))

    def invert(n, carry):
        some = pl.ds(pl.multiple_of(n * 96, 8), 96)
        inv[some, :] = 1.0 / (inv[some, :] + shift)
        return carry

    lax.fori_loop(0, J // 96, invert, 0)

    collect(TENSOR, t, lambda o: b_sum, b_all, bg_send, bg_recv)
    for n in range(TENSOR // 2):
        pair = jnp.concatenate([b_all[2 * n], b_all[2 * n + 1]], axis=0)
        b_lo[16 * n:16 * (n + 1), :] = pair.astype(bf16)[:, 0:J]

    lax.fori_loop(6, 8, own, 0)

    def left_core_wait(o, carry):
        remote(left.at[:, o, 1 - core], left.at[:, o, 1 - core], lc_send.at[o], lc_recv.at[o], d, t).wait_recv()
        return carry

    lax.fori_loop(0, X, left_core_wait, 0)

    collect(XC, xc, lambda o: a_sum, a_all, ag_send, ag_recv)
    for n in range(XC):
        a_full[8 * n:8 * (n + 1), :] = a_all[n]

    def ready(part):
        def arrived(k, carry):
            right_wait(flat(seq_of(k)))
            return carry

        def arrived_and_on(k, carry):
            s = flat(seq_of(k))
            right_wait(s)
            m = k - 8
            to_plane(s, jnp.where(m < 4, 3, 1), y_again.at[m]).start()
            return carry

        first = part * 4

        @pl.when(jnp.logical_and(part >= 2, part < 4))
        def _():
            lax.fori_loop(first, first + 4, arrived_and_on, 0)

        @pl.when(part >= 4)
        def _():
            lax.fori_loop(first, first + 4, arrived, 0)

    def cross(s, slot):
        wide = lax.dot_general(
            right[flat(s), :, 0:J], left[s[0], s[1], s[2]], FIRST_ROWS, preferred_element_type=f32
        )
        damped[slot] = (wide * inv[...]).astype(bf16)

    def project(slot):
        part = jnp.dot(b_lo[...], damped[slot], preferred_element_type=f32) * a_full[...]
        row = part[:, 0:128]
        for n in range(1, I // 128):
            row = row + part[:, n * 128:(n + 1) * 128]
        rows[slot] = row

    def score(of, slot):
        row = jnp.sum(rows[slot], axis=1, keepdims=True)
        lane = lax.broadcasted_iota(jnp.int32, (Q, 128), 1)
        scores[...] = jnp.where(lane == of, row, scores[...])

    def step(k, before, slot):
        s = seq_of(k)
        cross(s, slot)
        project(1 - slot)
        score(before[0], slot)
        return before[1], flat(s)

    scores[...] = jnp.zeros_like(scores)
    rows[...] = jnp.zeros_like(rows)
    damped[1] = jnp.zeros((J, I), bf16)

    def eighth(part, before):
        ready(part)

        def two(h, before):
            before = step(part * 4 + 2 * h, before, 0)
            return step(part * 4 + 2 * h + 1, before, 1)

        return lax.fori_loop(0, 2, two, before, unroll=True)

    before = lax.fori_loop(0, SEQS // 4, eighth, (-1, -1))
    project(1)
    score(before[0], 0)
    score(before[1], 1)

    by_seq = scores[...].T
    for n in range(ZH):
        f_part[n, :, 0:Q] = by_seq[8 * n:8 * (n + 1), :]
        f_part[n, :, Q:128] = jnp.zeros((8, 128 - Q), f32)
    spread(ZH, zh, lambda o: f_part.at[o], f_z, fz_send, fz_recv, in_zh)
    f_z[zh] = f_part[zh]
    collect(ZH, zh, lambda o: f_part.at[o], f_z, fz_send, fz_recv)
    f_mid[...] = (f_z[0] + f_z[1]) + (f_z[2] + f_z[3])
    spread(XC, xc, lambda o: f_mid, f_xc, fx_send, fx_recv, in_xc)
    f_xc[xc] = f_mid[...]
    collect(XC, xc, lambda o: f_mid, f_xc, fx_send, fx_recv)
    total = f_xc[0]
    for n in range(1, XC):
        total = total + f_xc[n]
    f_last[...] = total
    spread(TENSOR, t, lambda o: f_last, f_t, ft_send, ft_recv, in_t)
    f_t[t] = f_last[...]

    @pl.when(hop != 0)
    def _():
        lax.fori_loop(0, X, lambda quarter, carry: (right_z(quarter).wait_send(), carry)[1], 0)

    others(XC, xc, lambda o: right_x(o).wait_send())

    def sent_y(m, carry):
        to_plane(0, 1, y_send.at[0, m]).wait_send()
        to_plane(0, 1, y_send.at[1, m]).wait_send()
        to_plane(0, 1, y_again.at[m]).wait_send()
        return carry

    lax.fori_loop(0, 8, sent_y, 0)
    drain(TENSOR, t, lambda o: b_part.at[o], b_recv, b_send, b_rsem)
    drain(TENSOR, t, lambda o: b_sum, b_all, bg_send, bg_recv)
    drain(ZH, zh, lambda o: e_mine, e_z, ez_send, ez_recv)
    drain(XC, xc, lambda o: e_sum, e_xc, e_send, e_recv)
    drain(TENSOR, t, lambda o: e_mid, e_t, et_send, et_recv)
    drain(XC, xc, lambda o: a_part.at[o], a_xc, a_send, a_recv)
    drain(ZH, zh, lambda o: a_mid, a_z, az_send, az_recv)
    drain(XC, xc, lambda o: a_sum, a_all, ag_send, ag_recv)
    drain(ZH, zh, lambda o: f_part.at[o], f_z, fz_send, fz_recv)
    drain(XC, xc, lambda o: f_mid, f_xc, fx_send, fx_recv)
    others(ZH, zh, lambda o: left_z(o).wait_send())
    others(X, x, lambda o: left_x(o).wait_send())

    def sent_left_core(o, carry):
        left_core(o).wait_send()
        return carry

    lax.fori_loop(0, X, sent_left_core, 0)

    collect(TENSOR, t, lambda o: f_last, f_t, ft_send, ft_recv)
    total = f_t[0]
    for n in range(1, TENSOR):
        total = total + f_t[n]
    f_last_row = jnp.sum(
        jnp.where(lax.broadcasted_iota(jnp.int32, (8, 128), 0) == xc, total, 0.0), axis=0, keepdims=True
    )
    out_ref[...] = f_last_row[:, 0:Q]
    drain(TENSOR, t, lambda o: f_last, f_t, ft_send, ft_recv)


def on_device(
    query_acts, query_pos, query_feat, sae_enc, basis_in, basis_out, eigvals, train_in, train_out
):
    context = query_acts.shape[0]
    monitored = sae_enc.shape[0]
    vmem = pltpu.VMEM
    dma = pltpu.SemaphoreType.DMA
    scratch = [
        vmem((DIN // DP, context), bf16), vmem((monitored, DOUT // TENSOR), bf16),
        vmem((DIN // DP, I), bf16), vmem((J, DOUT // TENSOR), bf16), vmem((J, I), f32),
        vmem((R, DOUT), bf16),
        vmem((XC, R, JP), bf16), vmem((XC, R, JP), bf16), vmem((SEQS, R, JP), bf16), vmem((ZH, X, CORE, R, I), bf16),
        vmem((Q, J), f32), vmem((TENSOR, 8, JP), f32), vmem((TENSOR, 8, JP), f32), vmem((8, JP), f32),
        vmem((TENSOR, 8, JP), f32), vmem((Q, J), bf16),
        vmem((8, 128), f32), vmem((ZH, 8, 128), f32), vmem((8, 128), f32), vmem((XC, 8, 128), f32),
        vmem((8, 128), f32), vmem((TENSOR, 8, 128), f32),
        vmem((XC, 8, I), f32), vmem((XC, 8, I), f32), vmem((8, I), f32), vmem((ZH, 8, I), f32),
        vmem((8, I), f32), vmem((XC, 8, I), f32), vmem((Q, I), f32),
        vmem((2, J, I), bf16), vmem((2, Q, 128), f32), vmem((Q, 128), f32),
        vmem((ZH, 8, 128), f32), vmem((ZH, 8, 128), f32), vmem((8, 128), f32),
        vmem((XC, 8, 128), f32), vmem((8, 128), f32), vmem((TENSOR, 8, 128), f32),
        dma((7,)), dma((X,)), dma((X,)), dma((XC,)), dma((SEQS,)), dma((2, 8)), dma((8,)),
        dma((ZH,)), dma((ZH,)), dma((X,)), dma((X,)), dma((X,)), dma((X,)),
        dma((TENSOR,)), dma((TENSOR,)), dma((TENSOR,)), dma((TENSOR,)),
        dma((ZH,)), dma((ZH,)), dma((XC,)), dma((XC,)), dma((TENSOR,)), dma((TENSOR,)),
        dma((XC,)), dma((XC,)), dma((ZH,)), dma((ZH,)), dma((XC,)), dma((XC,)),
        dma((ZH,)), dma((ZH,)), dma((XC,)), dma((XC,)), dma((TENSOR,)), dma((TENSOR,)),
    ]
    anywhere = pl.BlockSpec(memory_space=pl.ANY)
    inside = pl.BlockSpec(memory_space=pltpu.VMEM)
    return pl.pallas_call(
        kernel,
        out_shape=jax.ShapeDtypeStruct((1, Q), f32),
        in_specs=[inside, inside] + [anywhere] * 7,
        out_specs=inside,
        scratch_shapes=scratch,
        compiler_params=pltpu.CompilerParams(
            collective_id=0, has_side_effects=True, vmem_limit_bytes=56 << 20
        ),
        name="influence",
    )(
        query_pos.reshape(1, Q), query_feat.reshape(1, Q), query_acts.T, sae_enc, basis_in, basis_out.T,
        eigvals.T, train_in.reshape(R, I), train_out.reshape(R, DOUT),
    ).reshape(Q, 1)


def solution(mesh):
    in_specs = (
        P(None, "dp"),
        P(),
        P(),
        P(None, "tensor"),
        P("dp", "tensor"),
        P("tensor", "dp"),
        P("tensor", "dp"),
        P("dp", None, "tensor"),
        P("dp", None, None),
    )
    out_specs = P(None, "dp")
    return jax.shard_map(
        on_device, mesh=mesh, in_specs=in_specs, out_specs=out_specs, check_vma=False
    )
```
